256 devices in a mesh: row: 8 (over y, core), col: 32 (over x, z).
Axes of the slice: x: 4, y: 4, z: 8, core: 2. Of those that a mesh axis runs over, the one named last changes fastest.
Arguments:
- left_factors: bfloat16 [16384, 4096], P('row', 'col'), may hold values from -0.125 to 0.125
- right_factors: bfloat16 [16384, 4096], P('row', 'col'), may hold values from -0.078125 to 0.078125
- closing_left: bfloat16 [2048, 4096], P(None, 'col'), may hold values from -0.125 to 0.125
- closing_right: bfloat16 [2048, 4096], P(None, 'col'), may hold values from -0.078125 to 0.078125
- panel_left: bfloat16 [16384, 128], P('row'), may hold values from -0.125 to 0.125
- panel_right: bfloat16 [16384, 128], P('row'), may hold values from -0.09375 to 0.09375
- diag_inverse: bfloat16 [16384, 2048], P('row'), may hold values from -1 to 2, as said below
- fronts: bfloat16 [16384, 4096], P('row', 'col'), may hold values from -6 to 6
Outputs:
- solved: float32 [16384, 4096], P('row', 'col')
- handoff: float32 [2048, 4096], P('row', 'col')
The draws below stay inside these ranges and needn't reach their ends.
Inputs may be any that keep to these rules, and one draw needn't show every extreme that they name: Each tile of diag_inverse is lower triangular with its diagonal between 0.5 and 2.
All inputs are finite; a program needn't handle non-finite values.
Results may differ from the reference program's by a relative error of at most 0.0012.
Values may be sent and summed in bfloat16 or wider, within the bound.
No kernel may reach another device: no remote copies, remote signals or barrier semaphores. Data moves between devices by JAX's collectives and lax.ppermute only.
A program may use at most 128 MiB of HBM per device.

```python
import math
import jax
import jax.numpy as jnp
from jax import lax

B = 2048
R = 128
SUB = 3
WROWS = 16384
FCOLS = 4096
N_ROW = 8
N_COL = 32


def draw_diag_inverse(key, part):
    key_off = jax.random.fold_in(key, 11)
    key_diag = jax.random.fold_in(key, 12)
    shape = (N_ROW, B, B)
    off = jax.random.normal(key_off, shape, jnp.float32) * (0.6 / math.sqrt(B))
    diag = jnp.exp(jax.random.uniform(key_diag, (N_ROW, B, 1), jnp.float32, math.log(0.5), math.log(2.0)))
    rowpos = lax.broadcasted_iota(jnp.int32, (B, B), 0)
    colpos = lax.broadcasted_iota(jnp.int32, (B, B), 1)
    below = (colpos < rowpos).astype(jnp.float32)
    onmain = (colpos == rowpos).astype(jnp.float32)
    full = off * below + diag * onmain
    return full.reshape(N_ROW * B, B).astype(jnp.bfloat16)


def steps_of(rng, shape, split, smallest, largest):
    def one(dim, parts):
        steps = jax.random.uniform(jax.random.fold_in(jax.random.fold_in(rng, 6), dim), (parts,), jnp.float32, smallest / len(split), largest / len(split))
        return jnp.repeat(jnp.exp(steps), shape[dim] // parts).reshape((-1,) + (1,) * (len(shape) - dim - 1))

    factor_of = one(*split[0])
    for cut in split[1:]:
        factor_of = factor_of * one(*cut)
    return factor_of


def normal_values(stream_key, extent, spread, bound, pieces=(), dtype=jnp.bfloat16):
    values = spread * jax.random.normal(stream_key, extent, jnp.float32)
    if pieces:
        values = values * steps_of(stream_key, extent, pieces, -0.22, 0.18)
    return jnp.clip(values, -bound, bound).astype(dtype)


def setup_inputs(seed: int = 0) -> dict:
    key_of = jax.random.split(jax.random.key(seed), 9)
    left_factors = normal_values(key_of[0], (WROWS, N_COL * R), B ** -0.5, 0.125, ((0, 8), (1, 32)))
    right_factors = normal_values(key_of[1], (WROWS, N_COL * R), (3 * B) ** -0.5, 0.078125, ((0, 8), (1, 32)))
    closing_left = normal_values(key_of[2], (B, N_COL * R), B ** -0.5, 0.125, ((1, 32),))
    closing_right = normal_values(key_of[3], (B, N_COL * R), (3 * B) ** -0.5, 0.078125, ((1, 32),))
    panel_left = normal_values(key_of[4], (WROWS, R), B ** -0.5, 0.125, ((0, 8),))
    panel_right = normal_values(key_of[5], (WROWS, R), (2 * B) ** -0.5, 0.09375, ((0, 8),))
    diag_inverse = draw_diag_inverse(jax.random.fold_in(key_of[8], 71), 0)
    fronts = normal_values(key_of[7], (WROWS, FCOLS), 1.0, 6.0, ((0, 8), (1, 32)))
    return {"left_factors": left_factors, "right_factors": right_factors, "closing_left": closing_left, "closing_right": closing_right, "panel_left": panel_left, "panel_right": panel_right, "diag_inverse": diag_inverse, "fronts": fronts}


HI = lax.Precision.HIGHEST

def orthonormal(image):
    gram = jnp.einsum('bs,bk->sk', image, image, precision=HI)
    lower = jnp.linalg.cholesky(gram)
    return jax.scipy.linalg.solve_triangular(lower, image.T, lower=True).T

def reference(left_factors, right_factors, closing_left, closing_right, panel_left, panel_right, diag_inverse, fronts):
    f32 = jnp.float32
    all_left = jnp.concatenate([left_factors, closing_left], 0).astype(f32).reshape(N_ROW + 1, B, N_COL, R)
    all_right = jnp.concatenate([right_factors, closing_right], 0).astype(f32).reshape(N_ROW + 1, B, N_COL, R)
    incoming = jnp.zeros((2 * R, FCOLS), f32)
    prev_left = jnp.zeros((B, 2 * R), jnp.bfloat16)
    solved_rows = []
    handoff_rows = []
    for row_at in range(N_ROW):
        cur = all_left[row_at]
        inner = jnp.einsum('bjr,bjs->jrs', all_right[row_at + 1], all_right[row_at], precision=HI)
        upd = jnp.einsum('bjr,jrs->bjs', all_left[row_at + 1], inner, precision=HI)
        dinv = diag_inverse[row_at * B:(row_at + 1) * B]
        right_here = panel_right[row_at * B:(row_at + 1) * B]
        left_here = panel_left[row_at * B:(row_at + 1) * B]
        basis = right_here.astype(f32)
        for turn in range(SUB):
            coeff = jnp.einsum('bjs,bk->jsk', cur, basis, precision=HI)
            image = jnp.einsum('bjs,jsk->bk', upd, coeff, precision=HI)
            ortho = orthonormal(image)
            back = jnp.einsum('bjs,bk->jsk', upd, ortho, precision=HI)
            basis = jnp.einsum('bjs,jsk->bk', cur, back, precision=HI)
        left_panel = jnp.concatenate([left_here, (-ortho).astype(jnp.bfloat16)], 1)
        right_panel = jnp.concatenate([right_here, basis.astype(jnp.bfloat16)], 1)
        weights = jnp.dot(dinv, right_panel, preferred_element_type=f32)
        direct = jnp.dot(dinv, fronts[row_at * B:(row_at + 1) * B], preferred_element_type=f32)
        carried = jnp.dot(dinv, prev_left, preferred_element_type=f32)
        result = direct - jnp.dot(carried, incoming, precision=HI)
        incoming = jnp.einsum('bk,bf->kf', weights, result, precision=HI)
        solved_rows.append(result)
        handoff_rows.append(incoming)
        prev_left = left_panel
    return (jnp.concatenate(solved_rows, 0), jnp.concatenate(handoff_rows, 0))
```

```python
import jax
import jax.numpy as jnp
from jax import lax
from jax.sharding import PartitionSpec as P

SUB = 3
NX, NZ = 4, 8

HI = lax.Precision.HIGHEST
f32, bf16, f16 = jnp.float32, jnp.bfloat16, jnp.float16

Z_GROUPS = [[x * NZ + z for z in range(NZ)] for x in range(NX)]
MATE = [(c, c ^ 1) for c in range(NX * NZ)]


def along_x(step):
    return [(c, (c // NZ + step) % NX * NZ + c % NZ) for c in range(NX * NZ)]


def along_z(step):
    return [(c, c // NZ * NZ + (c % NZ + 2 * step) % NZ) for c in range(NX * NZ)]


def from_behind(block, axis, distance):
    devices = range(lax.axis_size(axis))
    route = [(i - distance, i) for i in devices if i - distance in devices]
    return lax.ppermute(block, axis, route)


def total(block, route):
    got = [lax.ppermute(block, "col", route(d)) for d in (1, 2, 3)]
    return (block + got[2]) + (got[0] + got[1])


def gathered(block, route, place):
    near = [block] + [lax.ppermute(block, "col", route(d)) for d in (1, 2, 3)]
    line = jnp.concatenate(near[::-1] + near[:0:-1], 0)
    return lax.dynamic_slice_in_dim(line, (3 - place) * block.shape[0], 4 * block.shape[0], 0)


def split(value):
    high = lax.reduce_precision(value, 8, 7)
    return high.astype(bf16), (value - high).astype(bf16)


def inverse_factor(gram):
    lower = jnp.linalg.cholesky(gram)
    return lax.linalg.triangular_solve(lower, jnp.eye(gram.shape[0], dtype=f32), left_side=True, lower=True)


def update_block(left, right, next_left, next_right, x, z):
    order, rank = left.shape
    part = order // NX
    inner = lax.dot_general(next_right, right, (((0,), (0,)), ((), ())), preferred_element_type=f32)
    lefts = [left] + [lax.ppermute(left, "col", along_x(d)) for d in (1, 2, 3)]
    slices = [lax.dynamic_slice_in_dim(next_left, (x + d) % NX * part, part, 0) for d in range(NX)]
    slices = slices[:1] + [lax.ppermute(slices[d], "col", along_x(d)) for d in (1, 2, 3)]
    inners = [inner] + [lax.ppermute(inner, "col", along_x(d)) for d in (1, 2, 3)]
    upd = jnp.concatenate([jnp.dot(s.astype(f32), m, precision=HI) for s, m in zip(slices, inners)], 1)
    wide = jnp.concatenate(lefts, 1).reshape(NZ, order // NZ, NX * rank)
    power = jnp.floor(jnp.log2(512.0 / jnp.maximum(jnp.max(jnp.abs(upd)), 1e-30)))
    high, low = split(upd * jnp.exp2(power))
    dims = (((2,), (1,)), ((), ()))
    term = lax.dot_general(wide, high, dims, preferred_element_type=f32)
    term = term + lax.dot_general(wide, low, dims, preferred_element_type=f32)
    note = jnp.full((NZ, 16, part), power, f32)
    sent = jnp.concatenate([term, note], 1).astype(f16)
    got = lax.all_to_all(sent, "col", 0, 0, axis_index_groups=Z_GROUPS, tiled=True).astype(f32)
    rows = order // NZ
    mine = jnp.sum(got[:, :rows] * jnp.exp2(-got[:, rows:rows + 1, :1]), 0)
    other = lax.ppermute(mine, "col", MATE)
    even = z % 2 == 0
    return jnp.concatenate([jnp.where(even, mine, other), jnp.where(even, other, mine)], 0)


def recompress(block, start):
    part = block.shape[0]
    basis = start.astype(f32)
    factor = None
    for turn in range(SUB):
        image = total(lax.dot_general(block, basis, (((0,), (0,)), ((), ())), precision=HI), along_z)
        if factor is not None:
            image = lax.dot_general(image, factor, (((1,), (1,)), ((), ())), precision=HI)
        gram = lax.dot_general(image, image, (((0,), (0,)), ((), ())), precision=HI)
        back = jnp.dot(block, image, precision=HI)
        both = total(jnp.concatenate([back, gram], 0), along_x)
        basis, gram = both[:part], both[part:]
        factor = inverse_factor(gram)
    dims = (((1,), (1,)), ((), ()))
    ortho = lax.dot_general(image, factor, dims, precision=HI)
    return ortho, lax.dot_general(basis, factor, dims, precision=HI)


def local(
    left_factors,
    right_factors,
    closing_left,
    closing_right,
    panel_left,
    panel_right,
    diag_inverse,
    fronts,
):
    order, rank = panel_left.shape
    width = fronts.shape[1]
    part = order // 4
    rows_count = lax.axis_size("row")
    col = lax.axis_index("col")
    x, z = col // NZ, col % NZ
    got_left, got_right = from_behind((left_factors, right_factors), "row", -1)
    at_last = lax.axis_index("row") == rows_count - 1
    next_left = jnp.where(at_last, closing_left, got_left)
    next_right = jnp.where(at_last, closing_right, got_right)
    block = update_block(left_factors, right_factors, next_left, next_right, x, z)
    start = lax.dynamic_slice_in_dim(panel_right, z // 2 * part, part, 0)
    ortho, basis = recompress(block, start)
    prev_ortho = gathered(from_behind((-ortho).astype(bf16), "row", 1), along_x, x)
    prev_panel = from_behind(panel_left, "row", 1)
    full_basis = gathered(basis.astype(bf16), along_z, z // 2)
    fixed = jnp.dot(diag_inverse, jnp.concatenate([fronts, panel_right, prev_panel], 1), preferred_element_type=f32)
    late = jnp.dot(diag_inverse, jnp.concatenate([full_basis, prev_ortho], 1), preferred_element_type=f32)
    direct = fixed[:, :width]
    weights = jnp.concatenate([fixed[:, width:width + rank], late[:, :rank]], 1)
    carried = jnp.concatenate([fixed[:, width + rank:], late[:, rank:]], 1)
    seen = lax.dot_general(
        weights, jnp.concatenate([direct, carried], 1), (((0,), (0,)), ((), ())), precision=HI
    )
    offset, link = seen[:, :width], seen[:, width:]
    incoming = jnp.zeros((2 * rank, width), f32)
    for _ in range(rows_count - 1):
        incoming = from_behind(offset - jnp.dot(link, incoming, precision=HI), "row", 1)
    result = direct - jnp.dot(carried, incoming, precision=HI)
    return (result, offset - jnp.dot(link, incoming, precision=HI))


def solution(mesh):
    return jax.shard_map(
        local,
        mesh=mesh,
        in_specs=(
            P("row", "col"),
            P("row", "col"),
            P(None, "col"),
            P(None, "col"),
            P("row", None),
            P("row", None),
            P("row", None),
            P("row", "col"),
        ),
        out_specs=(P("row", "col"), P("row", "col")),
        check_vma=False,
    )
```

```python
import jax
import jax.numpy as jnp
from jax import lax
from jax.experimental import pallas as pl
from jax.experimental.pallas import tpu as pltpu
from jax.sharding import PartitionSpec as P

SUB = 3
NX, NZ = 4, 8
NOTE = 16

HI = lax.Precision.HIGHEST
f32, bf16, f16 = jnp.float32, jnp.bfloat16, jnp.float16

Z_GROUPS = [[x * NZ + z for z in range(NZ)] for x in range(NX)]
MATE = [(c, c ^ 1) for c in range(NX * NZ)]


def along_x(step):
    return [(c, (c // NZ + step) % NX * NZ + c % NZ) for c in range(NX * NZ)]


def along_z(step):
    return [(c, c // NZ * NZ + (c % NZ + 2 * step) % NZ) for c in range(NX * NZ)]


def across(up, step):
    columns = NX * NZ
    route = []
    for row in range(8):
        if up < 0 or row + up < 8:
            route += [(row * columns + a, (row + up) % 8 * columns + b) for a, b in along_x(step)]
    return route


def from_behind(block, axis, distance):
    devices = range(lax.axis_size(axis))
    route = [(i - distance, i) for i in devices if i - distance in devices]
    return lax.ppermute(block, axis, route)


def total(block, route):
    got = [lax.ppermute(block, "col", route(d)) for d in (2, 1, 3)]
    return (block + got[0]) + (got[1] + got[2])


def in_order(near, place):
    line = jnp.concatenate(near[::-1] + near[:0:-1], 0)
    size = near[0].shape[0]
    return lax.dynamic_slice_in_dim(line, (3 - place) * size, 4 * size, 0)


def inverse_factor_kernel(gram_ref, out_ref):
    size = gram_ref.shape[0]
    tiles = size // 8
    row = lax.broadcasted_iota(jnp.int32, (8, size), 0)
    lane = lax.broadcasted_iota(jnp.int32, (8, size), 1)
    left = [gram_ref[8 * i:8 * i + 8, :] for i in range(tiles)]
    right = [jnp.where(lane == row + 8 * i, 1.0, 0.0) for i in range(tiles)]
    for p in range(tiles):
        columns = [
            [jnp.broadcast_to(left[i][:, 8 * p + j:8 * p + j + 1], (8, size)) for i in range(p, tiles)]
            for j in range(8)
        ]
        scales = jnp.zeros((8, size), f32)
        for j in range(8):
            pivot = columns[j][0][j:j + 1, :]
            over = 1.0 / pivot
            scales = jnp.where(row == j, lax.rsqrt(pivot), scales)
            ratio = [c * over for c in columns[j]]
            for l in range(j + 1, 8):
                times = ratio[0][l:l + 1, :]
                columns[l] = [c - times * d for c, d in zip(columns[l], columns[j])]
            ratio[0] = jnp.where(row > j, ratio[0], 0.0)
            left_row, right_row = left[p][j:j + 1, :], right[p][j:j + 1, :]
            for i in range(p, tiles):
                left[i] = left[i] - ratio[i - p] * left_row
                right[i] = right[i] - ratio[i - p] * right_row
        out_ref[8 * p:8 * p + 8, :] = right[p] * scales


def inverse_factor(both, rank):
    return pl.pallas_call(
        inverse_factor_kernel,
        grid=(1,),
        in_specs=[pl.BlockSpec((rank, rank), lambda i: (both.shape[0] // rank - 1, 0))],
        out_specs=pl.BlockSpec((rank, rank), lambda i: (0, 0)),
        out_shape=jax.ShapeDtypeStruct((rank, rank), f32),
        cost_estimate=pl.CostEstimate(flops=40_000_000, bytes_accessed=131072, transcendentals=0),
    )(both)


def split(value):
    high = lax.reduce_precision(value, 8, 7)
    return high.astype(bf16), (value - high).astype(bf16)


def term_kernel(*refs):
    lefts, slices, inners, (out_ref, high_ref, low_ref, power_ref) = refs[:4], refs[4:8], refs[8:12], refs[12:]
    rows, rank = lefts[0].shape

    @pl.when(pl.program_id(0) == 0)
    def _():
        upd = [
            jnp.dot(s[...], m[:rank, :], preferred_element_type=f32)
            + jnp.dot(s[...], m[rank:, :], preferred_element_type=f32)
            for s, m in zip(slices, inners)
        ]
        top = [jnp.max(jnp.abs(u), axis=(0, 1), keepdims=True) for u in upd]
        top = jnp.maximum(jnp.maximum(top[0], top[1]), jnp.maximum(top[2], top[3]))
        power = jnp.floor(jnp.log(512.0 / jnp.maximum(top, 1e-30)) * 1.4426950408889634)
        power_ref[...] = jnp.broadcast_to(power, power_ref.shape)
        scale = jnp.exp(power * 0.6931471805599453)
        for d, u in enumerate(upd):
            value = u * scale
            high = value.astype(bf16)
            high_ref[:, d * rank:(d + 1) * rank] = high
            low_ref[:, d * rank:(d + 1) * rank] = (value - high.astype(f32)).astype(bf16)

    result = jnp.zeros((rows, high_ref.shape[0]), f32)
    for d, left in enumerate(lefts):
        for part_ref in (high_ref, low_ref):
            result += lax.dot_general(
                left[...], part_ref[:, d * rank:(d + 1) * rank], (((1,), (1,)), ((), ())), preferred_element_type=f32
            )
    out_ref[0, :rows, :] = result
    out_ref[0, rows:, :] = jnp.broadcast_to(power_ref[:1, :1], (NOTE, result.shape[1]))


def terms(packed, slices):
    part, rank = slices[0].shape
    order = packed[0].shape[0] - 2 * rank
    rows = order // NZ
    return pl.pallas_call(
        term_kernel,
        grid=(NZ,),
        in_specs=[pl.BlockSpec((rows, rank), lambda i: (i, 0))] * 4
        + [pl.BlockSpec((part, rank), lambda i: (0, 0))] * 4
        + [pl.BlockSpec((2 * rank, rank), lambda i: (order // (2 * rank), 0))] * 4,
        out_specs=pl.BlockSpec((1, rows + NOTE, part), lambda i: (i, 0, 0)),
        out_shape=jax.ShapeDtypeStruct((NZ, rows + NOTE, part), f32),
        scratch_shapes=[
            pltpu.VMEM((part, NX * rank), bf16),
            pltpu.VMEM((part, NX * rank), bf16),
            pltpu.VMEM((8, 128), f32),
        ],
        cost_estimate=pl.CostEstimate(flops=2 * 2 * order * part * NX * rank, bytes_accessed=8 << 20, transcendentals=0),
        compiler_params=pltpu.CompilerParams(vmem_limit_bytes=24 << 20),
    )(*packed, *slices, *packed)


def update_block(left, right, closing_left, closing_right, at_first, x, z):
    order, rank = left.shape
    part, rows = order // NX, order // NZ
    both = ("row", "col")
    next_right = lax.ppermute(jnp.where(at_first, closing_right, right), both, across(-1, 0))
    given = jnp.where(at_first, closing_left, left)
    slices = [lax.dynamic_slice_in_dim(given, (x + d) % NX * part, part, 0) for d in range(NX)]
    slices = [lax.ppermute(slices[d], both, across(-1, d)) for d in range(NX)]
    inner = lax.dot_general(next_right, right, (((0,), (0,)), ((), ())), preferred_element_type=f32)
    packed = jnp.concatenate([left, *split(inner)], 0)
    packed, *slices = lax.optimization_barrier((packed, *slices))
    packed = [packed] + [lax.ppermute(packed, "col", along_x(d)) for d in (1, 2, 3)]
    sent = terms(packed, slices).astype(f16)
    got = lax.all_to_all(sent, "col", 0, 0, axis_index_groups=Z_GROUPS, tiled=True).astype(f32)
    mine = jnp.sum(got[:, :rows] * jnp.exp2(-got[:, rows:rows + 1, :1]), 0)
    other = lax.ppermute(mine, "col", MATE)
    even = z % 2 == 0
    return jnp.concatenate([jnp.where(even, mine, other), jnp.where(even, other, mine)], 0)


def recompress(block, start):
    part = block.shape[0]
    basis = start.astype(f32)
    factor = None
    for turn in range(SUB):
        image = total(lax.dot_general(block, basis, (((0,), (0,)), ((), ())), precision=HI), along_z)
        if factor is not None:
            image = lax.dot_general(image, factor, (((1,), (1,)), ((), ())), precision=HI)
        gram = lax.dot_general(image, image, (((0,), (0,)), ((), ())), precision=HI)
        back = jnp.dot(block, image, precision=HI)
        both = total(jnp.concatenate([back, gram], 0), along_x)
        basis = both[:part]
        factor = inverse_factor(both, start.shape[1])
    dims = (((1,), (1,)), ((), ()))
    ortho = lax.dot_general(image, factor, dims, precision=HI)
    return ortho, lax.dot_general(basis, factor, dims, precision=HI)


def late_kernel(inverse_ref, basis_ref, ortho_ref, fixed_ref, carried_ref, seen_ref):
    rank = basis_ref.shape[1]
    width = fixed_ref.shape[1] - 2 * rank
    late = [jnp.dot(inverse_ref[...], r[...], preferred_element_type=f32) for r in (basis_ref, ortho_ref)]
    weights = [fixed_ref[:, width:width + rank], late[0]]
    carried = jnp.concatenate([fixed_ref[:, width + rank:], late[1]], 1)
    carried_ref[...] = carried
    right = jnp.concatenate([fixed_ref[:, :width], carried], 1)

    @pl.when(pl.program_id(0) == 0)
    def _():
        seen_ref[...] = jnp.zeros_like(seen_ref)

    for half, w in enumerate(weights):
        seen_ref[half * rank:(half + 1) * rank, :] += lax.dot_general(
            w, right, (((0,), (0,)), ((), ())), precision=HI, preferred_element_type=f32
        )


def late_products(inverse, basis, ortho, fixed):
    order, rank = basis.shape
    rows = order // 8
    wide = fixed.shape[1]
    return pl.pallas_call(
        late_kernel,
        grid=(8,),
        in_specs=[
            pl.BlockSpec((rows, order), lambda i: (i, 0)),
            pl.BlockSpec((order, rank), lambda i: (0, 0)),
            pl.BlockSpec((order, rank), lambda i: (0, 0)),
            pl.BlockSpec((rows, wide), lambda i: (i, 0)),
        ],
        out_specs=(
            pl.BlockSpec((rows, 2 * rank), lambda i: (i, 0)),
            pl.BlockSpec((2 * rank, wide), lambda i: (0, 0)),
        ),
        out_shape=(jax.ShapeDtypeStruct((order, 2 * rank), f32), jax.ShapeDtypeStruct((2 * rank, wide), f32)),
        cost_estimate=pl.CostEstimate(flops=4 << 30, bytes_accessed=12 << 20, transcendentals=0),
        compiler_params=pltpu.CompilerParams(vmem_limit_bytes=24 << 20),
    )(inverse, basis, ortho, fixed)


def local(
    left_factors,
    right_factors,
    closing_left,
    closing_right,
    panel_left,
    panel_right,
    diag_inverse,
    fronts,
):
    order, rank = panel_left.shape
    width = fronts.shape[1]
    part = order // 4
    col = lax.axis_index("col")
    x, z = col // NZ, col % NZ
    at_first = lax.axis_index("row") == 0
    block = update_block(left_factors, right_factors, closing_left, closing_right, at_first, x, z)
    start = lax.dynamic_slice_in_dim(panel_right, z // 2 * part, part, 0)
    ortho, basis = recompress(block, start)
    sent = (-ortho).astype(bf16)
    prev_ortho = in_order([lax.ppermute(sent, ("row", "col"), across(1, d)) for d in range(NX)], x)
    basis = basis.astype(bf16)
    full_basis = in_order([basis] + [lax.ppermute(basis, "col", along_z(d)) for d in (1, 2, 3)], z // 2)
    prev_panel = from_behind(panel_left, "row", 1)
    fixed = jnp.dot(diag_inverse, jnp.concatenate([fronts, panel_right, prev_panel], 1), preferred_element_type=f32)
    carried, seen = late_products(diag_inverse, full_basis, prev_ortho, fixed)
    direct = fixed[:, :width]
    offset, link = seen[:, :width], -seen[:, width:]
    short = link.astype(bf16)
    near = [(from_behind(short, "row", d), from_behind(offset, "row", d)) for d in (1, 2)]
    held = near[0][1] + jnp.dot(near[0][0].astype(f32), near[1][1], precision=HI)
    chain = jnp.dot(near[0][0], near[1][0], preferred_element_type=f32)
    far = (from_behind(chain.astype(bf16), "row", 2), from_behind(held, "row", 2))
    held = held + jnp.dot(chain, far[1], precision=HI)
    chain = jnp.dot(chain, far[0].astype(f32), precision=HI)
    incoming = held + jnp.dot(chain, from_behind(held, "row", 4), precision=HI)
    result = direct - jnp.dot(carried, incoming, precision=HI)
    return (result, offset + jnp.dot(link, incoming, precision=HI))


def solution(mesh):
    return jax.shard_map(
        local,
        mesh=mesh,
        in_specs=(
            P("row", "col"),
            P("row", "col"),
            P(None, "col"),
            P(None, "col"),
            P("row", None),
            P("row", None),
            P("row", None),
            P("row", "col"),
        ),
        out_specs=(P("row", "col"), P("row", "col")),
        check_vma=False,
    )
```

```python
import jax
import jax.numpy as jnp
from jax import lax
from jax.experimental import pallas as pl
from jax.experimental.pallas import tpu as pltpu
from jax.sharding import PartitionSpec as P

SUB = 3
NX, NZ = 4, 8
NOTE = 16

HI = lax.Precision.HIGHEST
f32, bf16, f16 = jnp.float32, jnp.bfloat16, jnp.float16

Z_GROUPS = [[x * NZ + z for z in range(NZ)] for x in range(NX)]
MATE = [(c, c ^ 1) for c in range(NX * NZ)]


def along_x(step):
    return [(c, (c // NZ + step) % NX * NZ + c % NZ) for c in range(NX * NZ)]


def along_z(step):
    return [(c, c // NZ * NZ + (c % NZ + 2 * step) % NZ) for c in range(NX * NZ)]


def across(up, step):
    columns = NX * NZ
    route = []
    for row in range(8):
        if up < 0 or row + up < 8:
            route += [(row * columns + a, (row + up) % 8 * columns + b) for a, b in along_x(step)]
    return route


def from_behind(block, axis, distance):
    devices = range(lax.axis_size(axis))
    route = [(i - distance, i) for i in devices if i - distance in devices]
    return lax.ppermute(block, axis, route)


def total(block, route):
    got = [lax.ppermute(block, "col", route(d)) for d in (2, 1, 3)]
    return (block + got[0]) + (got[1] + got[2])


def in_order(near, place):
    line = jnp.concatenate(near[::-1] + near[:0:-1], 0)
    size = near[0].shape[0]
    return lax.dynamic_slice_in_dim(line, (3 - place) * size, 4 * size, 0)


def inverse_factor_kernel(gram_ref, out_ref):
    size = gram_ref.shape[0]
    tiles = size // 8
    row = lax.broadcasted_iota(jnp.int32, (8, size), 0)
    lane = lax.broadcasted_iota(jnp.int32, (8, size), 1)
    left = [gram_ref[8 * i:8 * i + 8, :] for i in range(tiles)]
    right = [jnp.where(lane == row + 8 * i, 1.0, 0.0) for i in range(tiles)]
    for p in range(tiles):
        columns = [
            [jnp.broadcast_to(left[i][:, 8 * p + j:8 * p + j + 1], (8, size)) for i in range(p, tiles)]
            for j in range(8)
        ]
        scales = jnp.zeros((8, size), f32)
        for j in range(8):
            pivot = columns[j][0][j:j + 1, :]
            over = 1.0 / pivot
            scales = jnp.where(row == j, lax.rsqrt(pivot), scales)
            ratio = [c * over for c in columns[j]]
            for l in range(j + 1, 8):
                times = ratio[0][l:l + 1, :]
                columns[l] = [c - times * d for c, d in zip(columns[l], columns[j])]
            ratio[0] = jnp.where(row > j, ratio[0], 0.0)
            left_row, right_row = left[p][j:j + 1, :], right[p][j:j + 1, :]
            for i in range(p, tiles):
                left[i] = left[i] - ratio[i - p] * left_row
                right[i] = right[i] - ratio[i - p] * right_row
        out_ref[8 * p:8 * p + 8, :] = right[p] * scales


def inverse_factor(both, rank):
    return pl.pallas_call(
        inverse_factor_kernel,
        grid=(1,),
        in_specs=[pl.BlockSpec((rank, rank), lambda i: (both.shape[0] // rank - 1, 0))],
        out_specs=pl.BlockSpec((rank, rank), lambda i: (0, 0)),
        out_shape=jax.ShapeDtypeStruct((rank, rank), f32),
        cost_estimate=pl.CostEstimate(flops=40_000_000, bytes_accessed=131072, transcendentals=0),
    )(both)


def split(value):
    high = lax.reduce_precision(value, 8, 7)
    return high.astype(bf16), (value - high).astype(bf16)


def term_kernel(*refs):
    lefts, slices, inners, (out_ref, high_ref, low_ref, power_ref) = refs[:4], refs[4:8], refs[8:12], refs[12:]
    rows, rank = lefts[0].shape

    @pl.when(pl.program_id(0) == 0)
    def _():
        upd = [
            jnp.dot(s[...], m[:rank, :], preferred_element_type=f32)
            + jnp.dot(s[...], m[rank:, :], preferred_element_type=f32)
            for s, m in zip(slices, inners)
        ]
        top = [jnp.max(jnp.abs(u), axis=(0, 1), keepdims=True) for u in upd]
        top = jnp.maximum(jnp.maximum(top[0], top[1]), jnp.maximum(top[2], top[3]))
        power = jnp.floor(jnp.log(512.0 / jnp.maximum(top, 1e-30)) * 1.4426950408889634)
        power_ref[...] = jnp.broadcast_to(power, power_ref.shape)
        scale = jnp.exp(power * 0.6931471805599453)
        for d, u in enumerate(upd):
            value = u * scale
            high = value.astype(bf16)
            high_ref[:, d * rank:(d + 1) * rank] = high
            low_ref[:, d * rank:(d + 1) * rank] = (value - high.astype(f32)).astype(bf16)

    result = jnp.zeros((rows, high_ref.shape[0]), f32)
    for d, left in enumerate(lefts):
        for part_ref in (high_ref, low_ref):
            result += lax.dot_general(
                left[...], part_ref[:, d * rank:(d + 1) * rank], (((1,), (1,)), ((), ())), preferred_element_type=f32
            )
    out_ref[0, :rows, :] = result
    out_ref[0, rows:, :] = jnp.broadcast_to(power_ref[:1, :1], (NOTE, result.shape[1]))


def terms(lefts, inners, slices):
    part, rank = slices[0].shape
    order = NX * part
    rows = order // NZ

    def last(array):
        place = array.shape[0] // (2 * rank) - 1
        return pl.BlockSpec((2 * rank, rank), lambda i: (place, 0))

    return pl.pallas_call(
        term_kernel,
        grid=(NZ,),
        in_specs=[pl.BlockSpec((rows, rank), lambda i: (i, 0))] * 4
        + [pl.BlockSpec((part, rank), lambda i: (0, 0))] * 4
        + [last(m) for m in inners],
        out_specs=pl.BlockSpec((1, rows + NOTE, part), lambda i: (i, 0, 0)),
        out_shape=jax.ShapeDtypeStruct((NZ, rows + NOTE, part), f32),
        scratch_shapes=[
            pltpu.VMEM((part, NX * rank), bf16),
            pltpu.VMEM((part, NX * rank), bf16),
            pltpu.VMEM((8, 128), f32),
        ],
        cost_estimate=pl.CostEstimate(flops=2 * 2 * order * part * NX * rank, bytes_accessed=8 << 20, transcendentals=0),
        compiler_params=pltpu.CompilerParams(vmem_limit_bytes=24 << 20),
    )(*lefts, *slices, *inners)


def update_block(left, right, closing_left, closing_right, at_first, x):
    order, rank = left.shape
    part, rows = order // NX, order // NZ
    both = ("row", "col")
    next_right = lax.ppermute(jnp.where(at_first, closing_right, right), both, across(-1, 0))
    far = lax.ppermute(left, "col", along_x(2))
    given = jnp.where(at_first, closing_left, left)
    slices = [lax.dynamic_slice_in_dim(given, (x + d) % NX * part, part, 0) for d in range(NX)]
    slices = [lax.ppermute(slices[d], both, across(-1, d)) for d in range(NX)]
    inner = lax.dot_general(next_right, right, (((0,), (0,)), ((), ())), preferred_element_type=f32)
    inner = jnp.concatenate(split(inner), 0)
    packed = jnp.concatenate([left, inner], 0)
    packed, inner, far, *slices = lax.optimization_barrier((packed, inner, far, *slices))
    one, three = [lax.ppermute(packed, "col", along_x(d)) for d in (1, 3)]
    two = lax.ppermute(inner, "col", along_x(2))
    sent = terms((packed, one, far, three), (packed, one, two, three), slices).astype(f16)
    got = lax.all_to_all(sent, "col", 0, 0, axis_index_groups=Z_GROUPS, tiled=True).astype(f32)
    return jnp.sum(got[:, :rows] * jnp.exp2(-got[:, rows:rows + 1, :1]), 0)


def with_mate(half, even):
    other = lax.ppermute(half, "col", MATE)
    return jnp.concatenate([jnp.where(even, half, other), jnp.where(even, other, half)], 0)


def recompress(block, start, even):
    rows = block.shape[0]
    basis = start.astype(f32)
    factor = None
    for turn in range(SUB):
        image = lax.dot_general(block, basis, (((0,), (0,)), ((), ())), precision=HI)
        upper, lower = image[:rows], image[rows:]
        half = jnp.where(even, upper, lower) + lax.ppermute(jnp.where(even, lower, upper), "col", MATE)
        image = with_mate(total(half, along_z), even)
        if factor is not None:
            image = lax.dot_general(image, factor, (((1,), (1,)), ((), ())), precision=HI)
        gram = lax.dot_general(image, image, (((0,), (0,)), ((), ())), precision=HI)
        back = jnp.dot(block, image, precision=HI)
        both = total(jnp.concatenate([back, gram], 0), along_x)
        basis = both[:rows]
        factor = inverse_factor(both, start.shape[1])
    dims = (((1,), (1,)), ((), ()))
    ortho = lax.dot_general(image, factor, dims, precision=HI)
    return ortho, lax.dot_general(with_mate(basis, even), factor, dims, precision=HI)


def local(
    left_factors,
    right_factors,
    closing_left,
    closing_right,
    panel_left,
    panel_right,
    diag_inverse,
    fronts,
):
    order, rank = panel_left.shape
    width = fronts.shape[1]
    col = lax.axis_index("col")
    x, z = col // NZ, col % NZ
    at_first = lax.axis_index("row") == 0
    rows = order // NZ
    even = z % 2 == 0
    block = update_block(left_factors, right_factors, closing_left, closing_right, at_first, x)
    ortho, basis = recompress(block, lax.dynamic_slice_in_dim(panel_right, z * rows, rows, 0), even)
    sent = (-ortho).astype(bf16)
    prev_ortho = in_order([lax.ppermute(sent, ("row", "col"), across(1, d)) for d in range(NX)], x)
    basis = basis.astype(bf16)
    full_basis = in_order([basis] + [lax.ppermute(basis, "col", along_z(d)) for d in (1, 2, 3)], z // 2)
    prev_panel = from_behind(panel_left, "row", 1)
    fixed = jnp.dot(diag_inverse, jnp.concatenate([fronts, panel_right, prev_panel], 1), preferred_element_type=f32)
    late = jnp.dot(diag_inverse, jnp.concatenate([full_basis, prev_ortho], 1), preferred_element_type=f32)
    direct = fixed[:, :width]
    weights = jnp.concatenate([fixed[:, width:width + rank], late[:, :rank]], 1)
    carried = jnp.concatenate([fixed[:, width + rank:], late[:, rank:]], 1)
    seen = lax.dot_general(
        weights, jnp.concatenate([direct, carried], 1), (((0,), (0,)), ((), ())), precision=HI
    )
    offset, link = seen[:, :width], -seen[:, width:]
    short = link.astype(bf16)
    near = [(from_behind(short, "row", d), from_behind(offset, "row", d)) for d in (1, 2)]
    held = near[0][1] + jnp.dot(near[0][0].astype(f32), near[1][1], precision=HI)
    chain = jnp.dot(near[0][0], near[1][0], preferred_element_type=f32)
    far = (from_behind(chain.astype(bf16), "row", 2), from_behind(held, "row", 2))
    held = held + jnp.dot(chain, far[1], precision=HI)
    chain = jnp.dot(chain, far[0].astype(f32), precision=HI)
    incoming = held + jnp.dot(chain, from_behind(held, "row", 4), precision=HI)
    result = direct - jnp.dot(carried, incoming, precision=HI)
    return (result, offset + jnp.dot(link, incoming, precision=HI))


def solution(mesh):
    return jax.shard_map(
        local,
        mesh=mesh,
        in_specs=(
            P("row", "col"),
            P("row", "col"),
            P(None, "col"),
            P(None, "col"),
            P("row", None),
            P("row", None),
            P("row", None),
            P("row", "col"),
        ),
        out_specs=(P("row", "col"), P("row", "col")),
        check_vma=False,
    )
```

```python
import jax
import jax.numpy as jnp
from jax import lax
from jax.experimental import pallas as pl
from jax.experimental.pallas import tpu as pltpu
from jax.sharding import PartitionSpec as P

SUB = 3
NX, NZ = 4, 8
NOTE = 16

HI = lax.Precision.HIGHEST
f32, bf16, f16 = jnp.float32, jnp.bfloat16, jnp.float16

Z_GROUPS = [[x * NZ + z for z in range(NZ)] for x in range(NX)]
MATE = [(c, c ^ 1) for c in range(NX * NZ)]


def along_x(step):
    return [(c, (c // NZ + step) % NX * NZ + c % NZ) for c in range(NX * NZ)]


def along_z(step):
    return [(c, c // NZ * NZ + (c % NZ + 2 * step) % NZ) for c in range(NX * NZ)]


def across(up, step):
    columns = NX * NZ
    route = []
    for row in range(8):
        if up < 0 or row + up < 8:
            route += [(row * columns + a, (row + up) % 8 * columns + b) for a, b in along_x(step)]
    return route


def from_behind(block, axis, distance):
    devices = range(lax.axis_size(axis))
    route = [(i - distance, i) for i in devices if i - distance in devices]
    return lax.ppermute(block, axis, route)


def total(block, route):
    got = [lax.ppermute(block, "col", route(d)) for d in (2, 1, 3)]
    return (block + got[0]) + (got[1] + got[2])


def in_order(near, place):
    line = jnp.concatenate(near[::-1] + near[:0:-1], 0)
    size = near[0].shape[0]
    return lax.dynamic_slice_in_dim(line, (3 - place) * size, 4 * size, 0)


def inverse_factor_kernel(gram_ref, out_ref):
    size = gram_ref.shape[0]
    tiles = size // 8
    row = lax.broadcasted_iota(jnp.int32, (8, size), 0)
    lane = lax.broadcasted_iota(jnp.int32, (8, size), 1)
    left = [gram_ref[8 * i:8 * i + 8, :] for i in range(tiles)]
    right = [jnp.where(lane == row + 8 * i, 1.0, 0.0) for i in range(tiles)]
    for p in range(tiles):
        columns = [
            [jnp.broadcast_to(left[i][:, 8 * p + j:8 * p + j + 1], (8, size)) for i in range(p, tiles)]
            for j in range(8)
        ]
        scales = jnp.zeros((8, size), f32)
        for j in range(8):
            pivot = columns[j][0][j:j + 1, :]
            over = 1.0 / pivot
            scales = jnp.where(row == j, lax.rsqrt(pivot), scales)
            ratio = [c * over for c in columns[j]]
            for l in range(j + 1, 8):
                times = ratio[0][l:l + 1, :]
                columns[l] = [c - times * d for c, d in zip(columns[l], columns[j])]
            ratio[0] = jnp.where(row > j, ratio[0], 0.0)
            left_row, right_row = left[p][j:j + 1, :], right[p][j:j + 1, :]
            for i in range(p, tiles):
                left[i] = left[i] - ratio[i - p] * left_row
                right[i] = right[i] - ratio[i - p] * right_row
        out_ref[8 * p:8 * p + 8, :] = right[p] * scales


def inverse_factor(both, rank):
    return pl.pallas_call(
        inverse_factor_kernel,
        grid=(1,),
        in_specs=[pl.BlockSpec((rank, rank), lambda i: (both.shape[0] // rank - 1, 0))],
        out_specs=pl.BlockSpec((rank, rank), lambda i: (0, 0)),
        out_shape=jax.ShapeDtypeStruct((rank, rank), f32),
        cost_estimate=pl.CostEstimate(flops=40_000_000, bytes_accessed=131072, transcendentals=0),
    )(both)


def split(value):
    high = lax.reduce_precision(value, 8, 7)
    return high.astype(bf16), (value - high).astype(bf16)


def term_kernel(*refs):
    lefts, slices, inners, (out_ref, high_ref, low_ref, power_ref) = refs[:4], refs[4:8], refs[8:12], refs[12:]
    rows, rank = lefts[0].shape

    @pl.when(pl.program_id(0) == 0)
    def _():
        upd = [
            jnp.dot(s[...], m[:rank, :], preferred_element_type=f32)
            + jnp.dot(s[...], m[rank:, :], preferred_element_type=f32)
            for s, m in zip(slices, inners)
        ]
        top = [jnp.max(jnp.abs(u), axis=(0, 1), keepdims=True) for u in upd]
        top = jnp.maximum(jnp.maximum(top[0], top[1]), jnp.maximum(top[2], top[3]))
        power = jnp.floor(jnp.log(512.0 / jnp.maximum(top, 1e-30)) * 1.4426950408889634)
        power_ref[...] = jnp.broadcast_to(power, power_ref.shape)
        scale = jnp.exp(power * 0.6931471805599453)
        for d, u in enumerate(upd):
            value = u * scale
            high = value.astype(bf16)
            high_ref[:, d * rank:(d + 1) * rank] = high
            low_ref[:, d * rank:(d + 1) * rank] = (value - high.astype(f32)).astype(bf16)

    result = jnp.zeros((rows, high_ref.shape[0]), f32)
    for d, left in enumerate(lefts):
        for part_ref in (high_ref, low_ref):
            result += lax.dot_general(
                left[...], part_ref[:, d * rank:(d + 1) * rank], (((1,), (1,)), ((), ())), preferred_element_type=f32
            )
    out_ref[0, :rows, :] = result
    out_ref[0, rows:, :] = jnp.broadcast_to(power_ref[:1, :1], (NOTE, result.shape[1]))


def terms(lefts, inners, slices):
    part, rank = slices[0].shape
    order = NX * part
    rows = order // NZ

    def last(array):
        place = array.shape[0] // (2 * rank) - 1
        return pl.BlockSpec((2 * rank, rank), lambda i: (place, 0))

    return pl.pallas_call(
        term_kernel,
        grid=(NZ,),
        in_specs=[pl.BlockSpec((rows, rank), lambda i: (i, 0))] * 4
        + [pl.BlockSpec((part, rank), lambda i: (0, 0))] * 4
        + [last(m) for m in inners],
        out_specs=pl.BlockSpec((1, rows + NOTE, part), lambda i: (i, 0, 0)),
        out_shape=jax.ShapeDtypeStruct((NZ, rows + NOTE, part), f32),
        scratch_shapes=[
            pltpu.VMEM((part, NX * rank), bf16),
            pltpu.VMEM((part, NX * rank), bf16),
            pltpu.VMEM((8, 128), f32),
        ],
        cost_estimate=pl.CostEstimate(flops=2 * 2 * order * part * NX * rank, bytes_accessed=8 << 20, transcendentals=0),
        compiler_params=pltpu.CompilerParams(vmem_limit_bytes=24 << 20),
    )(*lefts, *slices, *inners)


def update_block(left, right, closing_left, closing_right, at_first, x, meanwhile):
    order, rank = left.shape
    part, rows = order // NX, order // NZ
    both = ("row", "col")
    next_right = lax.ppermute(jnp.where(at_first, closing_right, right), both, across(-1, 0))
    far = lax.ppermute(left, "col", along_x(2))
    given = jnp.where(at_first, closing_left, left)
    slices = [lax.dynamic_slice_in_dim(given, (x + d) % NX * part, part, 0) for d in range(NX)]
    slices = [lax.ppermute(slices[d], both, across(-1, d)) for d in range(NX)]
    inner = lax.dot_general(next_right, right, (((0,), (0,)), ((), ())), preferred_element_type=f32)
    inner = jnp.concatenate(split(inner), 0)
    packed = jnp.concatenate([left, inner], 0)
    packed, inner, far, *slices = lax.optimization_barrier((packed, inner, far, *slices))
    one, three = [lax.ppermute(packed, "col", along_x(d)) for d in (1, 3)]
    two = lax.ppermute(inner, "col", along_x(2))
    sent = terms((packed, one, far, three), (packed, one, two, three), slices).astype(f16)
    got = lax.all_to_all(sent, "col", 0, 0, axis_index_groups=Z_GROUPS, tiled=True)
    got, other = lax.optimization_barrier((got, meanwhile(sent)))
    got = got.astype(f32)
    return jnp.sum(got[:, :rows] * jnp.exp2(-got[:, rows:rows + 1, :1]), 0), other


def with_mate(half, even):
    other = lax.ppermute(half, "col", MATE)
    return jnp.concatenate([jnp.where(even, half, other), jnp.where(even, other, half)], 0)


def recompress(block, start, even):
    rows = block.shape[0]
    basis = start.astype(f32)
    factor = None
    for turn in range(SUB):
        image = lax.dot_general(block, basis, (((0,), (0,)), ((), ())), precision=HI)
        upper, lower = image[:rows], image[rows:]
        half = jnp.where(even, upper, lower) + lax.ppermute(jnp.where(even, lower, upper), "col", MATE)
        if factor is not None:
            half, factor = lax.optimization_barrier((half, factor))
        image = with_mate(total(half, along_z), even)
        if factor is not None:
            image = lax.dot_general(image, factor, (((1,), (1,)), ((), ())), precision=HI)
        gram = lax.dot_general(image, image, (((0,), (0,)), ((), ())), precision=HI)
        back = jnp.dot(block, image, precision=HI)
        both = total(jnp.concatenate([back, gram], 0), along_x)
        basis, both = lax.optimization_barrier((both[:rows], both))
        factor = inverse_factor(both, start.shape[1])
    dims = (((1,), (1,)), ((), ()))
    ortho = lax.dot_general(image, factor, dims, precision=HI)
    return ortho, lax.dot_general(with_mate(basis, even), factor, dims, precision=HI)


def local(
    left_factors,
    right_factors,
    closing_left,
    closing_right,
    panel_left,
    panel_right,
    diag_inverse,
    fronts,
):
    order, rank = panel_left.shape
    width = fronts.shape[1]
    col = lax.axis_index("col")
    x, z = col // NZ, col % NZ
    at_first = lax.axis_index("row") == 0
    rows = order // NZ
    even = z % 2 == 0

    def fixed_products(after):
        inverse, panel, _ = lax.optimization_barrier((diag_inverse, panel_left, after))
        right = jnp.concatenate([fronts, panel_right, from_behind(panel, "row", 1)], 1)
        return jnp.dot(inverse, right, preferred_element_type=f32)

    block, fixed = update_block(
        left_factors, right_factors, closing_left, closing_right, at_first, x, fixed_products
    )
    ortho, basis = recompress(block, lax.dynamic_slice_in_dim(panel_right, z * rows, rows, 0), even)
    sent = (-ortho).astype(bf16)
    prev_ortho = in_order([lax.ppermute(sent, ("row", "col"), across(1, d)) for d in range(NX)], x)
    basis = basis.astype(bf16)
    full_basis = in_order([basis] + [lax.ppermute(basis, "col", along_z(d)) for d in (1, 2, 3)], z // 2)
    late = jnp.dot(diag_inverse, jnp.concatenate([full_basis, prev_ortho], 1), preferred_element_type=f32)
    direct = fixed[:, :width]
    weights = jnp.concatenate([fixed[:, width:width + rank], late[:, :rank]], 1)
    carried = jnp.concatenate([fixed[:, width + rank:], late[:, rank:]], 1)
    seen = lax.dot_general(
        weights, jnp.concatenate([direct, carried], 1), (((0,), (0,)), ((), ())), precision=HI
    )
    offset, link = seen[:, :width], -seen[:, width:]
    short = link.astype(bf16)
    near = [(from_behind(short, "row", d), from_behind(offset, "row", d)) for d in (1, 2)]
    held = near[0][1] + jnp.dot(near[0][0].astype(f32), near[1][1], precision=HI)
    chain = jnp.dot(near[0][0], near[1][0], preferred_element_type=f32)
    far = (from_behind(chain.astype(bf16), "row", 2), from_behind(held, "row", 2))
    held = held + jnp.dot(chain, far[1], precision=HI)
    chain = jnp.dot(chain, far[0].astype(f32), precision=HI)
    incoming = held + jnp.dot(chain, from_behind(held, "row", 4), precision=HI)
    result = direct - jnp.dot(carried, incoming, precision=HI)
    return (result, offset + jnp.dot(link, incoming, precision=HI))


def solution(mesh):
    return jax.shard_map(
        local,
        mesh=mesh,
        in_specs=(
            P("row", "col"),
            P("row", "col"),
            P(None, "col"),
            P(None, "col"),
            P("row", None),
            P("row", None),
            P("row", None),
            P("row", "col"),
        ),
        out_specs=(P("row", "col"), P("row", "col")),
        check_vma=False,
    )
```

```python
import jax
import jax.numpy as jnp
from jax import lax
from jax.experimental import pallas as pl
from jax.experimental.pallas import tpu as pltpu
from jax.sharding import PartitionSpec as P

SUB = 3
NX, NZ = 4, 8
NOTE = 16

HI = lax.Precision.HIGHEST
f32, bf16, f16 = jnp.float32, jnp.bfloat16, jnp.float16

Z_GROUPS = [[x * NZ + z for z in range(NZ)] for x in range(NX)]
MATE = [(c, c ^ 1) for c in range(NX * NZ)]


def along_x(step):
    return [(c, (c // NZ + step) % NX * NZ + c % NZ) for c in range(NX * NZ)]


def along_z(step):
    return [(c, c // NZ * NZ + (c % NZ + 2 * step) % NZ) for c in range(NX * NZ)]


def across(up, step):
    columns = NX * NZ
    route = []
    for row in range(8):
        if up < 0 or row + up < 8:
            route += [(row * columns + a, (row + up) % 8 * columns + b) for a, b in along_x(step)]
    return route


def from_behind(block, axis, distance):
    devices = range(lax.axis_size(axis))
    route = [(i - distance, i) for i in devices if i - distance in devices]
    return lax.ppermute(block, axis, route)


def total(block, route):
    got = [lax.ppermute(block, "col", route(d)) for d in (2, 1, 3)]
    return (block + got[0]) + (got[1] + got[2])


def in_order(near, place):
    line = jnp.concatenate(near[::-1] + near[:0:-1], 0)
    size = near[0].shape[0]
    return lax.dynamic_slice_in_dim(line, (3 - place) * size, 4 * size, 0)


def inverse_factor_kernel(gram_ref, out_ref):
    size = gram_ref.shape[0]
    tiles = size // 8
    row = lax.broadcasted_iota(jnp.int32, (8, size), 0)
    lane = lax.broadcasted_iota(jnp.int32, (8, size), 1)
    left = [gram_ref[8 * i:8 * i + 8, :] for i in range(tiles)]
    right = [jnp.where(lane == row + 8 * i, 1.0, 0.0) for i in range(tiles)]
    for p in range(tiles):
        columns = [
            [jnp.broadcast_to(left[i][:, 8 * p + j:8 * p + j + 1], (8, size)) for i in range(p, tiles)]
            for j in range(8)
        ]
        scales = jnp.zeros((8, size), f32)
        for j in range(8):
            pivot = columns[j][0][j:j + 1, :]
            over = 1.0 / pivot
            scales = jnp.where(row == j, lax.rsqrt(pivot), scales)
            ratio = [c * over for c in columns[j]]
            for l in range(j + 1, 8):
                times = ratio[0][l:l + 1, :]
                columns[l] = [c - times * d for c, d in zip(columns[l], columns[j])]
            ratio[0] = jnp.where(row > j, ratio[0], 0.0)
            left_row, right_row = left[p][j:j + 1, :], right[p][j:j + 1, :]
            for i in range(p, tiles):
                left[i] = left[i] - ratio[i - p] * left_row
                right[i] = right[i] - ratio[i - p] * right_row
        out_ref[8 * p:8 * p + 8, :] = right[p] * scales


def inverse_factor(both, rank):
    return pl.pallas_call(
        inverse_factor_kernel,
        grid=(1,),
        in_specs=[pl.BlockSpec((rank, rank), lambda i: (both.shape[0] // rank - 1, 0))],
        out_specs=pl.BlockSpec((rank, rank), lambda i: (0, 0)),
        out_shape=jax.ShapeDtypeStruct((rank, rank), f32),
        cost_estimate=pl.CostEstimate(flops=40_000_000, bytes_accessed=131072, transcendentals=0),
    )(both)


def split(value):
    high = lax.reduce_precision(value, 8, 7)
    return high.astype(bf16), (value - high).astype(bf16)


def term_kernel(*refs):
    lefts, slices, inners, (out_ref, high_ref, low_ref, power_ref) = refs[:4], refs[4:8], refs[8:12], refs[12:]
    rows, rank = lefts[0].shape

    @pl.when(pl.program_id(0) == 0)
    def _():
        upd = [
            jnp.dot(s[...], m[:rank, :], preferred_element_type=f32)
            + jnp.dot(s[...], m[rank:, :], preferred_element_type=f32)
            for s, m in zip(slices, inners)
        ]
        top = [jnp.max(jnp.abs(u), axis=(0, 1), keepdims=True) for u in upd]
        top = jnp.maximum(jnp.maximum(top[0], top[1]), jnp.maximum(top[2], top[3]))
        power = jnp.floor(jnp.log(512.0 / jnp.maximum(top, 1e-30)) * 1.4426950408889634)
        power_ref[...] = jnp.broadcast_to(power, power_ref.shape)
        scale = jnp.exp(power * 0.6931471805599453)
        for d, u in enumerate(upd):
            value = u * scale
            high = value.astype(bf16)
            high_ref[:, d * rank:(d + 1) * rank] = high
            low_ref[:, d * rank:(d + 1) * rank] = (value - high.astype(f32)).astype(bf16)

    result = jnp.zeros((rows, high_ref.shape[0]), f32)
    for d, left in enumerate(lefts):
        for part_ref in (high_ref, low_ref):
            result += lax.dot_general(
                left[...], part_ref[:, d * rank:(d + 1) * rank], (((1,), (1,)), ((), ())), preferred_element_type=f32
            )
    out_ref[0, :rows, :] = result
    out_ref[0, rows:, :] = jnp.broadcast_to(power_ref[:1, :1], (NOTE, result.shape[1]))


def terms(lefts, inners, slices):
    part, rank = slices[0].shape
    order = NX * part
    rows = order // NZ

    def last(array):
        place = array.shape[0] // (2 * rank) - 1
        return pl.BlockSpec((2 * rank, rank), lambda i: (place, 0))

    return pl.pallas_call(
        term_kernel,
        grid=(NZ,),
        in_specs=[pl.BlockSpec((rows, rank), lambda i: (i, 0))] * 4
        + [pl.BlockSpec((part, rank), lambda i: (0, 0))] * 4
        + [last(m) for m in inners],
        out_specs=pl.BlockSpec((1, rows + NOTE, part), lambda i: (i, 0, 0)),
        out_shape=jax.ShapeDtypeStruct((NZ, rows + NOTE, part), f32),
        scratch_shapes=[
            pltpu.VMEM((part, NX * rank), bf16),
            pltpu.VMEM((part, NX * rank), bf16),
            pltpu.VMEM((8, 128), f32),
        ],
        cost_estimate=pl.CostEstimate(flops=2 * 2 * order * part * NX * rank, bytes_accessed=8 << 20, transcendentals=0),
        compiler_params=pltpu.CompilerParams(vmem_limit_bytes=24 << 20),
    )(*lefts, *slices, *inners)


def update_block(left, right, closing_left, closing_right, at_first, x, meanwhile):
    order, rank = left.shape
    part, rows = order // NX, order // NZ
    both = ("row", "col")
    next_right = lax.ppermute(jnp.where(at_first, closing_right, right), both, across(-1, 0))
    far = lax.ppermute(left, "col", along_x(2))
    given = jnp.where(at_first, closing_left, left)
    slices = [lax.dynamic_slice_in_dim(given, (x + d) % NX * part, part, 0) for d in range(NX)]
    slices = [lax.ppermute(slices[d], both, across(-1, d)) for d in range(NX)]
    inner = lax.dot_general(next_right, right, (((0,), (0,)), ((), ())), preferred_element_type=f32)
    inner = jnp.concatenate(split(inner), 0)
    packed = jnp.concatenate([left, inner], 0)
    packed, inner, far, *slices = lax.optimization_barrier((packed, inner, far, *slices))
    one, three = [lax.ppermute(packed, "col", along_x(d)) for d in (1, 3)]
    two = lax.ppermute(inner, "col", along_x(2))
    sent = terms((packed, one, far, three), (packed, one, two, three), slices).astype(f16)
    got = lax.all_to_all(sent, "col", 0, 0, axis_index_groups=Z_GROUPS, tiled=True)
    got, other = lax.optimization_barrier((got, meanwhile(sent)))
    got = got.astype(f32)
    return jnp.sum(got[:, :rows] * jnp.exp2(-got[:, rows:rows + 1, :1]), 0), other


def with_mate(half, even):
    other = lax.ppermute(half, "col", MATE)
    return jnp.concatenate([jnp.where(even, half, other), jnp.where(even, other, half)], 0)


def recompress(block, start, even):
    rows = block.shape[0]
    basis = start.astype(f32)
    factor = None
    for turn in range(SUB):
        image = lax.dot_general(block, basis, (((0,), (0,)), ((), ())), precision=HI)
        upper, lower = image[:rows], image[rows:]
        half = jnp.where(even, upper, lower) + lax.ppermute(jnp.where(even, lower, upper), "col", MATE)
        if factor is not None:
            half, factor = lax.optimization_barrier((half, factor))
        image = with_mate(total(half, along_z), even)
        if factor is not None:
            image = lax.dot_general(image, factor, (((1,), (1,)), ((), ())), precision=HI)
        gram = lax.dot_general(image, image, (((0,), (0,)), ((), ())), precision=HI)
        back = jnp.dot(block, image, precision=HI)
        both = total(jnp.concatenate([back, gram], 0), along_x)
        basis, both = lax.optimization_barrier((both[:rows], both))
        factor = inverse_factor(both, start.shape[1])
    dims = (((1,), (1,)), ((), ()))
    ortho = lax.dot_general(image, factor, dims, precision=HI)
    return ortho, lax.dot_general(with_mate(basis, even), factor, dims, precision=HI)


def local(
    left_factors,
    right_factors,
    closing_left,
    closing_right,
    panel_left,
    panel_right,
    diag_inverse,
    fronts,
):
    order, rank = panel_left.shape
    width = fronts.shape[1]
    col = lax.axis_index("col")
    x, z = col // NZ, col % NZ
    at_first = lax.axis_index("row") == 0
    rows = order // NZ
    even = z % 2 == 0

    def fixed_products(after):
        inverse, panel, _ = lax.optimization_barrier((diag_inverse, panel_left, after))
        right = jnp.concatenate([fronts, panel_right, from_behind(panel, "row", 1)], 1)
        return jnp.dot(inverse, right, preferred_element_type=f32)

    block, fixed = update_block(
        left_factors, right_factors, closing_left, closing_right, at_first, x, fixed_products
    )
    ortho, basis = recompress(block, lax.dynamic_slice_in_dim(panel_right, z * rows, rows, 0), even)
    sent = (-ortho).astype(bf16)
    prev_ortho = in_order([lax.ppermute(sent, ("row", "col"), across(1, d)) for d in range(NX)], x)
    basis = basis.astype(bf16)
    full_basis = in_order([basis] + [lax.ppermute(basis, "col", along_z(d)) for d in (1, 2, 3)], z // 2)
    late = jnp.dot(diag_inverse, jnp.concatenate([full_basis, prev_ortho], 1), preferred_element_type=f32)
    direct = fixed[:, :width]
    weights = jnp.concatenate([fixed[:, width:width + rank], late[:, :rank]], 1)
    carried = jnp.concatenate([fixed[:, width + rank:], late[:, rank:]], 1)
    seen = lax.dot_general(
        weights, jnp.concatenate([direct, carried], 1), (((0,), (0,)), ((), ())), precision=HI
    )
    offset, link = seen[:, :width], -seen[:, width:]
    def maps(chain, held, distances):
        packed = jnp.concatenate([chain.astype(bf16), *split(held)], 1)
        got = [from_behind(packed, "row", d) for d in distances]
        return [(g[:, :2 * rank], g[:, 2 * rank:-width].astype(f32) + g[:, -width:].astype(f32)) for g in got]

    near, next_near = maps(link, offset, (1, 2))
    held = near[1] + jnp.dot(near[0].astype(f32), next_near[1], precision=HI)
    chain = jnp.dot(near[0], next_near[0], preferred_element_type=f32)
    far, = maps(chain, held, (2,))
    held = held + jnp.dot(chain, far[1], precision=HI)
    chain = jnp.dot(chain, far[0].astype(f32), precision=HI)
    incoming = held + jnp.dot(chain, from_behind(held, "row", 4), precision=HI)
    result = direct - jnp.dot(carried, incoming, precision=HI)
    return (result, offset + jnp.dot(link, incoming, precision=HI))


def solution(mesh):
    return jax.shard_map(
        local,
        mesh=mesh,
        in_specs=(
            P("row", "col"),
            P("row", "col"),
            P(None, "col"),
            P(None, "col"),
            P("row", None),
            P("row", None),
            P("row", None),
            P("row", "col"),
        ),
        out_specs=(P("row", "col"), P("row", "col")),
        check_vma=False,
    )
```
